256 devices in a mesh: row: 4 (over z_lo, core), col: 16 (over z_hi, x), dp: 4 (over y).
Axes of the slice: x: 4, y: 4, z: 8 (z_hi: 4, z_lo: 2; z = z_hi * 2 + z_lo), core: 2. Of those that a mesh axis runs over, the one named last changes fastest.
Arguments:
- activations: bfloat16 [1536, 12288], P(('col', 'dp'), 'row'), may hold values from -6 to 6
- in_tiles: bfloat16 [4, 16, 8, 256, 256], P('row', 'col'), may hold values from -0.21875 to 0.21875
- out_tiles: bfloat16 [4, 16, 8, 256, 256], P('row', 'col'), may hold values from -0.15625 to 0.15625
- block_slots: int32 [4, 16, 8], P('row', 'col'), may hold values from -1 to 71, as said below
- out_cotangent: bfloat16 [1536, 12288], P(('col', 'dp'), 'row'), may hold values from -6 to 6
Outputs:
- layer_out: bfloat16 [1536, 12288], P(('col', 'dp'), 'row')
- act_grad: bfloat16 [1536, 12288], P(('col', 'dp'), 'row')
- in_tile_grad: bfloat16 [4, 16, 8, 256, 256], P('row', 'col')
- out_tile_grad: bfloat16 [4, 16, 8, 256, 256], P('row', 'col')
The draws below stay inside these ranges and needn't reach their ends.
Inputs may be any that keep to these rules, and one draw needn't show every extreme that they name: `block_slots`: in each cell the used slots come first and name distinct blocks of the cell's 12 x 6 blocks by the code (block row) * 6 + (block column); the remaining slots hold -1. Some cell uses all 8 slots.
All inputs are finite; a program needn't handle non-finite values.
Results may differ from the reference program's by a relative error of at most 0.035.
Values may be sent and summed in bfloat16 or wider, within the bound.
No kernel may reach another device: no remote copies, remote signals or barrier semaphores. Data moves between devices by JAX's collectives and lax.ppermute only.
A program may use at most 64 MiB of HBM per device.

```python
import jax
import jax.numpy as jnp
from jax import lax

D = 12288
FF = 24576
BLK = 256
CAP = 8
GRID_ROWS = 4
GRID_COLS = 16
D_BLOCKS = 12
F_BLOCKS = 6
TOKENS = 1536
N_ROW = 4
N_COL = 16


def draw_block_slots(key, part):
    key = jax.random.fold_in(key, 7)
    key_light, key_crowd, key_pick, key_order = jax.random.split(key, 4)
    cell_total = GRID_ROWS * GRID_COLS
    block_total = D_BLOCKS * F_BLOCKS
    light = jax.random.randint(key_light, (cell_total,), max(CAP // 4, 1), CAP // 2 + 1)
    chosen = jax.random.randint(key_pick, (), 0, cell_total)
    crowded = (jax.random.randint(key_crowd, (cell_total,), 0, 8) == 0) | (jnp.arange(cell_total) == chosen)
    filled = jnp.where(crowded, CAP, light)
    orders = jax.vmap(lambda sub_key: jax.random.permutation(sub_key, block_total))(jax.random.split(key_order, cell_total))
    top_code = block_total - 1
    chosen_row = orders[chosen]
    where_top = jnp.argmax(chosen_row == top_code)
    leading = chosen_row[0]
    fixed_row = chosen_row.at[where_top].set(leading).at[0].set(top_code)
    orders = orders.at[chosen].set(fixed_row)
    slot_codes = jnp.where(jnp.arange(CAP)[None, :] < filled[:, None], orders[:, :CAP], -1)
    return slot_codes.reshape(GRID_ROWS, GRID_COLS, CAP).astype(jnp.int32)


def steps_of(rng, shape, cuts, least, top_value):
    gain, own = 1.0, jax.random.fold_in(rng, 6)
    for axis_at, shards_of in cuts:
        steps = jnp.exp(jax.random.uniform(jax.random.fold_in(own, axis_at), (shards_of,), jnp.float32, least / len(cuts), top_value / len(cuts)))
        gain = gain * jnp.repeat(steps, shape[axis_at] // shards_of).reshape([-1 if axis == axis_at else 1 for axis in range(len(shape))])
    return gain


def noise(own_key, extent, spread, reach, shards=(), kind=jnp.bfloat16):
    factor_of = steps_of(own_key, extent, shards, -0.22, 0.18) if shards else 1.0
    values = jax.random.normal(own_key, extent, jnp.float32) * spread * factor_of
    return jnp.minimum(jnp.maximum(values, -reach), reach).astype(kind)


def setup_inputs(seed: int = 0) -> dict:
    key_list = jax.random.split(jax.random.key(seed), 6)
    activations = noise(key_list[0], (TOKENS, D), 1.0, 6.0, ((0, 64), (1, 4)))
    in_tiles = noise(key_list[1], (GRID_ROWS, GRID_COLS, CAP, BLK, BLK), (N_ROW * CAP * BLK // (2 * F_BLOCKS)) ** -0.5, 0.21875, ((0, 4), (1, 16)))
    out_tiles = noise(key_list[2], (GRID_ROWS, GRID_COLS, CAP, BLK, BLK), (N_COL * CAP * BLK // (2 * D_BLOCKS)) ** -0.5, 0.15625, ((0, 4), (1, 16)))
    block_slots = draw_block_slots(jax.random.fold_in(key_list[5], 71), 0)
    out_cotangent = noise(key_list[4], (TOKENS, D), 1.0, 6.0, ((0, 64), (1, 4)))
    return dict(activations=activations, in_tiles=in_tiles, out_tiles=out_tiles, block_slots=block_slots, out_cotangent=out_cotangent)


highest = lax.Precision.HIGHEST

def slot_tables(slot_codes):
    usable = slot_codes >= 0
    block_row = jnp.where(usable, slot_codes // F_BLOCKS, 0).astype(jnp.int32)
    block_col = jnp.where(usable, slot_codes % F_BLOCKS, 0).astype(jnp.int32)
    row_select = ((block_row[:, None] == jnp.arange(D_BLOCKS, dtype=jnp.int32)[None, :]) & usable[:, None]).astype(jnp.float32)
    col_select = ((block_col[:, None] == jnp.arange(F_BLOCKS, dtype=jnp.int32)[None, :]) & usable[:, None]).astype(jnp.float32)
    return (usable, block_row, block_col, row_select, col_select)

def picked(matrix, slot_index):
    return jnp.take(matrix.reshape(matrix.shape[0], -1, BLK), slot_index, axis=1).astype(jnp.float32)

def placed(product, select):
    return jnp.einsum('tsb,sk->tkb', product, select, precision=highest).reshape(product.shape[0], -1)

def masked(tile_set, usable):
    return jnp.where(usable[:, None, None], tile_set.astype(jnp.float32), jnp.float32(0.0))

def smooth_gate(values):
    return jax.nn.gelu(values, approximate=True)

def rounded(term):
    return lax.optimization_barrier(term.astype(jnp.bfloat16)).astype(jnp.float32)

def add_into(running, term, first_col, span_cols):
    before = lax.dynamic_slice_in_dim(running, first_col, span_cols, 1)
    return lax.dynamic_update_slice_in_dim(running, before + rounded(term), first_col, 1)

def reference(activations, in_tiles, out_tiles, block_slots, out_cotangent):
    token_rows = activations.shape[0]
    feature_span = D_BLOCKS * BLK
    hidden_span = F_BLOCKS * BLK
    cell_total = GRID_ROWS * GRID_COLS
    code_table = block_slots.reshape(cell_total, CAP)
    in_table = in_tiles.reshape(cell_total, CAP, BLK, BLK)
    out_table = out_tiles.reshape(cell_total, CAP, BLK, BLK)
    cell_ids = jnp.arange(cell_total, dtype=jnp.int32)

    def locate(cell_id):
        feature_start = (cell_id // GRID_COLS * feature_span).astype(jnp.int32)
        hidden_start = (cell_id % GRID_COLS * hidden_span).astype(jnp.int32)
        return (feature_start, hidden_start)

    def hidden_step(running, cell_id):
        feature_start, hidden_start = locate(cell_id)
        usable, block_row, block_col, row_select, col_select = slot_tables(code_table[cell_id])
        inputs = lax.dynamic_slice_in_dim(activations, feature_start, feature_span, 1)
        product = jnp.einsum('tsd,sdf->tsf', picked(inputs, block_row), masked(in_table[cell_id], usable), precision=highest)
        return (add_into(running, placed(product, col_select), hidden_start, hidden_span), None)
    hidden = lax.scan(hidden_step, jnp.zeros((token_rows, FF), jnp.float32), cell_ids)[0]
    gate_act = smooth_gate(hidden).astype(jnp.bfloat16)

    def output_step(running, cell_id):
        feature_start, hidden_start = locate(cell_id)
        usable, block_row, block_col, row_select, col_select = slot_tables(code_table[cell_id])
        source = lax.dynamic_slice_in_dim(gate_act, hidden_start, hidden_span, 1)
        product = jnp.einsum('tsf,sfd->tsd', picked(source, block_col), masked(out_table[cell_id], usable), precision=highest)
        return (add_into(running, placed(product, row_select), feature_start, feature_span), None)
    layer_out = lax.scan(output_step, jnp.zeros((token_rows, D), jnp.float32), cell_ids)[0].astype(jnp.bfloat16)

    def back_step(running, cell_id):
        feature_start, hidden_start = locate(cell_id)
        usable, block_row, block_col, row_select, col_select = slot_tables(code_table[cell_id])
        source = lax.dynamic_slice_in_dim(out_cotangent, feature_start, feature_span, 1)
        product = jnp.einsum('tsd,sfd->tsf', picked(source, block_row), masked(out_table[cell_id], usable), precision=highest)
        return (add_into(running, placed(product, col_select), hidden_start, hidden_span), None)
    gate_grad = lax.scan(back_step, jnp.zeros((token_rows, FF), jnp.float32), cell_ids)[0]
    hidden_grad = jax.vjp(smooth_gate, hidden)[1](gate_grad)[0].astype(jnp.bfloat16)

    def input_step(running, cell_id):
        feature_start, hidden_start = locate(cell_id)
        usable, block_row, block_col, row_select, col_select = slot_tables(code_table[cell_id])
        source = lax.dynamic_slice_in_dim(hidden_grad, hidden_start, hidden_span, 1)
        product = jnp.einsum('tsf,sdf->tsd', picked(source, block_col), masked(in_table[cell_id], usable), precision=highest)
        return (add_into(running, placed(product, row_select), feature_start, feature_span), None)
    act_grad = lax.scan(input_step, jnp.zeros((token_rows, D), jnp.float32), cell_ids)[0].astype(jnp.bfloat16)

    def tile_step(carry, cell_id):
        feature_start, hidden_start = locate(cell_id)
        usable, block_row, block_col, row_select, col_select = slot_tables(code_table[cell_id])
        inputs = lax.dynamic_slice_in_dim(activations, feature_start, feature_span, 1)
        cot_part = lax.dynamic_slice_in_dim(out_cotangent, feature_start, feature_span, 1)
        gate_part = lax.dynamic_slice_in_dim(gate_act, hidden_start, hidden_span, 1)
        grad_part = lax.dynamic_slice_in_dim(hidden_grad, hidden_start, hidden_span, 1)
        in_term = jnp.einsum('tsd,tsf->sdf', picked(inputs, block_row), picked(grad_part, block_col), precision=highest)
        out_term = jnp.einsum('tsf,tsd->sfd', picked(gate_part, block_col), picked(cot_part, block_row), precision=highest)
        keep_mask = usable[:, None, None]
        in_term = jnp.where(keep_mask, in_term, jnp.float32(0.0)).astype(jnp.bfloat16)
        out_term = jnp.where(keep_mask, out_term, jnp.float32(0.0)).astype(jnp.bfloat16)
        return (carry, (in_term, out_term))
    tile_pair = lax.scan(tile_step, jnp.float32(0.0), cell_ids)[1]
    in_tile_grad = tile_pair[0].reshape(GRID_ROWS, GRID_COLS, CAP, BLK, BLK)
    out_tile_grad = tile_pair[1].reshape(GRID_ROWS, GRID_COLS, CAP, BLK, BLK)
    return (layer_out, act_grad, in_tile_grad, out_tile_grad)
```

```python
import functools

import jax
import jax.numpy as jnp
from jax import lax
from jax.experimental import pallas as pl
from jax.experimental.pallas import tpu as pltpu
from jax.sharding import PartitionSpec as P

BLK = 256
CAP = 8
D_BLOCKS = 12
F_BLOCKS = 6
ROWS = 384
GROUP = 96
PART = 24
F32 = jnp.float32
BF16 = jnp.bfloat16

VMEM = pl.BlockSpec(memory_space=pltpu.VMEM)
SMEM = pl.BlockSpec(memory_space=pltpu.SMEM)
GROUP_ROWS = (GROUP, GROUP, GROUP, GROUP // 2, GROUP // 2)
LIMIT = 48 * 1024 * 1024


def swap_core(v):
    return lax.ppermute(v, "row", [(i, i ^ 1) for i in range(4)])


def swap_z(v):
    return lax.ppermute(v, "row", [(i, i ^ 2) for i in range(4)])


def x_to(v, k):
    return lax.ppermute(v, "col", [(i, i // 4 * 4 + (i + k) % 4) for i in range(16)])


def z_to(v, k):
    return lax.ppermute(v, "col", [(i, (i + 4 * k) % 16) for i in range(16)])


def y_to(v, k):
    return lax.ppermute(v, "dp", [(i, (i + k) % 4) for i in range(4)])


def gather_z(v):
    before, after, across = z_to(v, 1), z_to(v, -1), z_to(v, 2)
    return jnp.concatenate([v, before, after, across], axis=0)


def gather_x(own):
    half = GROUP // 2
    left, right = x_to(own, 1), x_to(own, -1)
    across_a = x_to(left[:half], 1)
    across_b = x_to(right[half:], -1)
    return own, left, right, across_a, across_b


def add(*terms):
    return functools.reduce(jnp.add, [t.astype(F32) for t in terms])


def scatter_x(groups):
    half = GROUP // 2
    own, left, right, across_a, across_b = groups
    from_left = x_to(across_a, 1)
    from_right = x_to(across_b, -1)
    right = jnp.concatenate([add(right[:half], from_left).astype(BF16), right[half:]], axis=0)
    left = jnp.concatenate([left[:half], add(left[half:], from_right).astype(BF16)], axis=0)
    return add(own, x_to(right, 1), x_to(left, -1)).astype(BF16)


def scatter_z(total):
    own, before, after, across = (total[i * PART : (i + 1) * PART] for i in range(4))
    return add(own, z_to(before, -1), z_to(after, 1), z_to(across, 2)).astype(BF16)


def dot(a, b, contract):
    return lax.dot_general(a, b, (contract, ((), ())), preferred_element_type=F32)


def pick(refs, block):
    at = pl.ds(pl.multiple_of(block * BLK, BLK), BLK)
    return jnp.concatenate([ref[:, at] for ref in refs], axis=0)


def call(body, outs, scratch, ins, n_smem, flops, moved):
    return pl.pallas_call(
        body,
        out_shape=[jax.ShapeDtypeStruct(s, BF16) for s in outs],
        in_specs=[SMEM] * n_smem + [VMEM] * (len(ins) - n_smem),
        out_specs=[VMEM] * len(outs),
        scratch_shapes=scratch,
        compiler_params=pltpu.CompilerParams(vmem_limit_bytes=LIMIT),
        cost_estimate=pl.CostEstimate(flops=flops, bytes_accessed=moved, transcendentals=0),
    )(*ins)


FLOPS = 2 * CAP * ROWS * BLK * BLK


def to_hidden(meta, groups, tiles, features_first):
    def body(meta_ref, a, b, c, d, e, tiles_ref, keep_ref, send_ref, acc):
        acc[...] = jnp.zeros_like(acc)
        for s in range(CAP):
            code = meta_ref[s]

            @pl.when(code >= 0)
            def _():
                x = pick((a, b, c, d, e), code // F_BLOCKS)
                at = pl.ds(pl.multiple_of(code % F_BLOCKS * BLK, BLK), BLK)
                acc[:, at] += dot(x, tiles_ref[s], ((1,), (0 if features_first else 1,)))

        core, half = meta_ref[CAP], ROWS // 2
        keep_ref[...] = acc[pl.ds(pl.multiple_of(core * half, half), half), :].astype(BF16)
        send_ref[...] = acc[pl.ds(pl.multiple_of((1 - core) * half, half), half), :].astype(BF16)

    shape = (ROWS // 2, F_BLOCKS * BLK)
    return call(
        body, [shape, shape], [pltpu.VMEM((ROWS, F_BLOCKS * BLK), F32)],
        (meta, *groups, tiles), 1, FLOPS, 5 * 1024 * 1024,
    )


def fill_panel(panel, meta_ref, mine, other):
    core, half = meta_ref[CAP], ROWS // 2
    panel[pl.ds(pl.multiple_of(core * half, half), half), :] = mine[...]
    panel[pl.ds(pl.multiple_of((1 - core) * half, half), half), :] = other[...]


PANEL = pltpu.VMEM((ROWS, F_BLOCKS * BLK), BF16)


def to_features(meta, mine, other, tiles, hidden_first):
    def body(meta_ref, mine_ref, other_ref, tiles_ref, a, b, c, d, e, panel, acc):
        fill_panel(panel, meta_ref, mine_ref, other_ref)
        acc[...] = jnp.zeros_like(acc)
        for s in range(CAP):
            code = meta_ref[s]

            @pl.when(code >= 0)
            def _():
                x = pick((panel,), code % F_BLOCKS)
                at = pl.ds(pl.multiple_of(code // F_BLOCKS * BLK, BLK), BLK)
                acc[:, at] += dot(x, tiles_ref[s], ((1,), (0 if hidden_first else 1,)))

        first = 0
        for ref, rows in zip((a, b, c, d, e), GROUP_ROWS):
            ref[...] = acc[first : first + rows, :].astype(BF16)
            first += rows

    return call(
        body, [(rows, D_BLOCKS * BLK) for rows in GROUP_ROWS],
        [PANEL, pltpu.VMEM((ROWS, D_BLOCKS * BLK), F32)],
        (meta, mine, other, tiles), 1, FLOPS, 5 * 1024 * 1024,
    )


def to_tiles(meta, groups, mine, other, features_first):
    def body(meta_ref, a, b, c, d, e, mine_ref, other_ref, o0, o1, o2, o3, panel):
        fill_panel(panel, meta_ref, mine_ref, other_ref)
        for k, ref in enumerate((o0, o1, o2, o3)):
            for j in range(2):
                code = meta_ref[(meta_ref[CAP + 1] + k) % 4 * 2 + j]

                @pl.when(code >= 0)
                def _():
                    x = pick((a, b, c, d, e), code // F_BLOCKS)
                    h = pick((panel,), code % F_BLOCKS)
                    pair = (x, h) if features_first else (h, x)
                    ref[j] = dot(*pair, ((0,), (0,))).astype(BF16)

                @pl.when(code < 0)
                def _():
                    ref[j] = jnp.zeros((BLK, BLK), BF16)

    return call(
        body, [(2, BLK, BLK)] * 4, [PANEL], (meta, *groups, mine, other), 1, FLOPS, 5 * 1024 * 1024
    )


def in_order(meta, parts):
    def body(meta_ref, p0, p1, p2, p3, out_ref):
        for k, ref in enumerate((p0, p1, p2, p3)):
            out_ref[pl.ds((meta_ref[CAP + 1] + 4 - k) % 4 * 2, 2)] = ref[...]

    return call(body, [(CAP, BLK, BLK)], [], (meta, *parts), 1, 0, 2 * 1024 * 1024)[0]


def sum_dp(meta, chunks):
    c0, c1, c2, c3 = chunks
    total = add(c0, y_to(c1, 1), y_to(c2, 2), y_to(c3, 3)).astype(BF16)
    return in_order(meta, (total, y_to(total, 1), y_to(total, 2), y_to(total, 3)))


def smooth_gate(values):
    return jax.nn.gelu(values, approximate=True)


def sum_row(keep, send):
    pair = add(keep, swap_core(send)).astype(BF16)
    return add(pair, swap_z(pair))


def per_device(activations, in_tiles, out_tiles, block_slots, out_cotangent):
    meta = jnp.concatenate(
        [
            block_slots[0, 0],
            jnp.stack([lax.axis_index("row") % 2, lax.axis_index("dp")]).astype(jnp.int32),
        ]
    )
    in_tiles, out_tiles = in_tiles[0, 0], out_tiles[0, 0]

    acts = gather_x(gather_z(activations))
    hidden = sum_row(*to_hidden(meta, acts, in_tiles, True))
    gate = smooth_gate(hidden).astype(BF16)
    gate_other = swap_core(gate)
    layer_out = scatter_z(scatter_x(to_features(meta, gate, gate_other, out_tiles, True)))

    cots = gather_x(gather_z(out_cotangent))
    gate_grad = sum_row(*to_hidden(meta, cots, out_tiles, False))
    out_grad = sum_dp(meta, to_tiles(meta, cots, gate, gate_other, False))
    hidden_grad = jax.vjp(smooth_gate, hidden)[1](gate_grad)[0].astype(BF16)
    grad_other = swap_core(hidden_grad)
    act_grad = scatter_z(scatter_x(to_features(meta, hidden_grad, grad_other, in_tiles, False)))
    in_grad = sum_dp(meta, to_tiles(meta, acts, hidden_grad, grad_other, True))
    return layer_out, act_grad, in_grad[None, None], out_grad[None, None]


def solution(mesh):
    in_specs = (
        P(("col", "dp"), "row"),
        P("row", "col", None, None, None),
        P("row", "col", None, None, None),
        P("row", "col", None),
        P(("col", "dp"), "row"),
    )
    out_specs = (
        P(("col", "dp"), "row"),
        P(("col", "dp"), "row"),
        P("row", "col", None, None, None),
        P("row", "col", None, None, None),
    )
    return jax.shard_map(
        per_device, mesh=mesh, in_specs=in_specs, out_specs=out_specs, check_vma=False
    )
```

```python
import functools

import jax
import jax.numpy as jnp
import numpy as np
from jax import lax
from jax.experimental import pallas as pl
from jax.experimental.pallas import tpu as pltpu
from jax.sharding import PartitionSpec as P

BLK = 256
CAP = 8
D_BLOCKS = 12
F_BLOCKS = 6
ROWS = 384
GROUP = 96
HALF = 48
PART = 24
WIDE = D_BLOCKS * BLK
HIDDEN = F_BLOCKS * BLK
F32 = jnp.float32
BF16 = jnp.bfloat16

VMEM = pl.BlockSpec(memory_space=pltpu.VMEM)
SMEM = pl.BlockSpec(memory_space=pltpu.SMEM)
ANY = pl.BlockSpec(memory_space=pl.ANY)
LIMIT = 48 * 1024 * 1024


def swap_core(halves):
    return [lax.ppermute(v, "row", [(i, i ^ 1) for i in range(4)]) for v in halves]


def swap_z(halves):
    return [lax.ppermute(v, "row", [(i, i ^ 2) for i in range(4)]) for v in halves]


def x_to(v, k):
    return lax.ppermute(v, "col", [(i, i // 4 * 4 + (i + k) % 4) for i in range(16)])


def z_to(v, k):
    return lax.ppermute(v, "col", [(i, (i + 4 * k) % 16) for i in range(16)])


def y_to(v, k):
    return lax.ppermute(v, "dp", [(i, (i + k) % 4) for i in range(4)])


def add(*terms):
    return functools.reduce(jnp.add, [t.astype(F32) for t in terms])


def gather_z(v):
    before, after, across = z_to(v, 1), z_to(v, -1), z_to(v, 2)
    return jnp.concatenate([v, before, after, across], axis=0)


def gather_x(own):
    left, right = x_to(own, 1), x_to(own, -1)
    return own, left, right, x_to(left[:HALF], 1), x_to(right[HALF:], -1)


def scatter_x(own, left, right, across_a, across_b):
    to_left, to_right = relay(left, right, x_to(across_a, 1), x_to(across_b, -1))
    return own, x_to(to_right, 1), x_to(to_left, -1)


def scatter_z(own, before, after, across):
    return add(own, z_to(before, -1), z_to(after, 1), z_to(across, 2)).astype(BF16)


def sum_dp(chunks):
    return add(*(y_to(c, k) if k else c for k, c in enumerate(chunks))).astype(BF16)


def spread_dp(table, total):
    before, after = y_to(total, 1), y_to(total, -1)
    return in_order(table, (total, before, after, y_to(before[:2], 1), y_to(after[2:], -1)))


def dot(a, b, contract):
    return lax.dot_general(a, b, (contract, ((), ())), preferred_element_type=F32)


def pick(windows, block):
    at = pl.ds(pl.multiple_of(block * BLK, BLK), BLK)
    return jnp.concatenate([ref[first : first + rows, at] for ref, first, rows in windows], axis=0)


def call(body, outs, scratch, ins, after=(), table=True):
    def run(*refs):
        body(*refs[: len(ins)], *refs[len(ins) + len(after) :])

    return pl.pallas_call(
        run,
        out_shape=[jax.ShapeDtypeStruct(s, BF16) for s in outs],
        in_specs=[SMEM] * table + [VMEM] * (len(ins) - table) + [ANY] * len(after),
        out_specs=[VMEM] * len(outs),
        scratch_shapes=scratch,
        compiler_params=pltpu.CompilerParams(vmem_limit_bytes=LIMIT),
        cost_estimate=pl.CostEstimate(flops=0, bytes_accessed=0, transcendentals=0),
    )(*ins, *after)


def windows(refs):
    return [(ref, 0, ref.shape[0]) for ref in refs]


def quarter(table_ref, i):
    return pl.ds(pl.multiple_of((table_ref[CAP + 1] * 2 + i) % 4 * GROUP, GROUP), GROUP)


def to_hidden(table, panel, tiles, features_first, after=()):
    n = len(panel)

    def body(table_ref, *refs):
        rows, tiles_ref, out_refs, acc = windows(refs[:n]), refs[n], refs[n + 1 : -1], refs[-1]
        acc[...] = jnp.zeros_like(acc)
        for s in range(CAP):
            code = table_ref[s]

            @pl.when(code >= 0)
            def _():
                x = pick(rows, code // F_BLOCKS)
                at = pl.ds(pl.multiple_of(code % F_BLOCKS * BLK, BLK), BLK)
                acc[:, at] += dot(x, tiles_ref[s], ((1,), (0 if features_first else 1,)))

        for i, ref in enumerate(out_refs):
            ref[...] = acc[quarter(table_ref, i), :].astype(BF16)

    return call(
        body, [(GROUP, HIDDEN)] * 4, [pltpu.VMEM((ROWS, HIDDEN), F32)], (table, *panel, tiles), after
    )


PANEL = pltpu.VMEM((ROWS, HIDDEN), BF16)


def fill_panel(panel, table_ref, quarters):
    for i, ref in enumerate(quarters):
        panel[quarter(table_ref, i), :] = ref[...]


def features(table_ref, quarters, tiles_ref, panel, acc, hidden_first):
    fill_panel(panel, table_ref, quarters)
    acc[...] = jnp.zeros_like(acc)
    for s in range(CAP):
        code = table_ref[s]

        @pl.when(code >= 0)
        def _():
            x = pick([(panel, 0, ROWS)], code % F_BLOCKS)
            at = pl.ds(pl.multiple_of(code // F_BLOCKS * BLK, BLK), BLK)
            acc[:, at] += dot(x, tiles_ref[s], ((1,), (0 if hidden_first else 1,)))


ACROSS = (GROUP, GROUP, GROUP, HALF, HALF)


def to_features(table, quarters, tiles, hidden_first, rows=ACROSS, after=()):
    def body(table_ref, *refs):
        out_refs, panel, acc = refs[5:-2], refs[-2], refs[-1]
        features(table_ref, refs[:4], refs[4], panel, acc, hidden_first)
        first = 0
        for ref, n in zip(out_refs, rows):
            ref[...] = acc[first : first + n, :].astype(BF16)
            first += n

    return call(
        body, [(n, WIDE) for n in rows], [PANEL, pltpu.VMEM((ROWS, WIDE), F32)],
        (table, *quarters, tiles), after,
    )


def relay(left, right, from_left, from_right):
    def body(left_ref, right_ref, from_left_ref, from_right_ref, to_left, to_right):
        to_right[:HALF, :] = add(right_ref[:HALF, :], from_left_ref[...]).astype(BF16)
        to_right[HALF:, :] = right_ref[HALF:, :]
        to_left[:HALF, :] = left_ref[:HALF, :]
        to_left[HALF:, :] = add(left_ref[HALF:, :], from_right_ref[...]).astype(BF16)

    return call(body, [(GROUP, WIDE)] * 2, [], (left, right, from_left, from_right), (), False)


def pack(out_total, *terms):
    def body(out_ref, t0, t1, t2, *packed):
        out = out_ref[...].astype(F32)
        act = add(t0[...], t1[...], t2[...])
        for i, ref in enumerate(packed):
            ref[0] = out[i * PART : (i + 1) * PART].astype(BF16)
            ref[1] = act[i * PART : (i + 1) * PART].astype(BF16)

    return call(body, [(2, PART, WIDE)] * 4, [], (out_total, *terms), (), False)


def tile(table_ref, s, rows, panel_ref, features_first, put):
    code = table_ref[s]

    @pl.when(code >= 0)
    def _():
        x = pick(rows, code // F_BLOCKS)
        h = pick([(panel_ref, 0, ROWS)], code % F_BLOCKS)
        pair = (x, h) if features_first else (h, x)
        put(dot(*pair, ((0,), (0,))).astype(BF16))

    @pl.when(code < 0)
    def _():
        put(jnp.zeros((BLK, BLK), BF16))


def to_out_tiles(table, panel, quarters, after):
    n = len(panel)

    def body(table_ref, *refs):
        out_ref, panel_ref = refs[-2:]
        fill_panel(panel_ref, table_ref, refs[n : n + 4])
        for s in range(CAP):
            tile(table_ref, s, windows(refs[:n]), panel_ref, False, functools.partial(out_ref.__setitem__, s))

    return call(body, [(CAP, BLK, BLK)], [PANEL], (table, *panel, *quarters), after)[0]


def to_in_tiles(table, panel, quarters, out_tiles, after):
    n = len(panel)

    def body(table_ref, *refs):
        out_tiles_ref, chunks, panel_ref = refs[n + 4], refs[n + 5 : -1], refs[-1]
        fill_panel(panel_ref, table_ref, refs[n : n + 4])
        for k, ref in enumerate(chunks):
            first = (table_ref[CAP] + k) % 4 * 2
            ref[:2] = out_tiles_ref[pl.ds(first, 2)]
            for j in range(2):
                tile(table_ref, first + j, windows(refs[:n]), panel_ref, True, functools.partial(ref.__setitem__, 2 + j))

    return call(body, [(4, BLK, BLK)] * 4, [PANEL], (table, *panel, *quarters, out_tiles), after)


def in_order(table, parts):
    def body(table_ref, own, before, after, across_out, across_in, out_grad, in_grad):
        def at(k):
            return pl.ds((table_ref[CAP] + k) % 4 * 2, 2)

        for k, ref in ((0, own), (3, before), (1, after)):
            out_grad[at(k)] = ref[:2]
            in_grad[at(k)] = ref[2:]
        out_grad[at(2)] = across_out[...]
        in_grad[at(2)] = across_in[...]

    return call(body, [(CAP, BLK, BLK)] * 2, [], (table, *parts))


A = (2.0 / np.pi) ** 0.5
B = 0.044715


def gated(pair, other):
    def body(*refs):
        for a, b, out in zip(refs[:2], refs[2:4], refs[4:]):
            v = add(a[...], b[...])
            out[...] = (0.5 * v * (1.0 + jnp.tanh(A * (v + B * v * v * v)))).astype(BF16)

    return call(body, [(GROUP, HIDDEN)] * 2, [], (*pair, *other), (), False)


def ungated(pair, other, back_pair, back_other, after):
    def body(*refs):
        for a, b, c, d, out in zip(refs[:2], refs[2:4], refs[4:6], refs[6:8], refs[8:]):
            v, g = add(a[...], b[...]), add(c[...], d[...])
            t = jnp.tanh(A * (v + B * v * v * v))
            slope = 0.5 * (1.0 + t) + 0.5 * v * (1.0 - t * t) * (A * (1.0 + 3.0 * B * v * v))
            out[...] = (g * slope).astype(BF16)

    ins = *pair, *other, *back_pair, *back_other
    return call(body, [(GROUP, HIDDEN)] * 2, [], ins, after, False)


def chip_sum(quarters):
    arrived = swap_core(quarters[2:])
    return [add(a, b).astype(BF16) for a, b in zip(quarters, arrived)]


def after(value, *others):
    return lax.optimization_barrier((value, others))[0]


def per_device(activations, in_tiles, out_tiles, block_slots, out_cotangent):
    places = jnp.stack([lax.axis_index("dp"), lax.axis_index("row") % 2]).astype(jnp.int32)
    table = jnp.concatenate([block_slots[0, 0], places])
    in_tiles, out_tiles = in_tiles[0, 0], out_tiles[0, 0]

    near = gather_z(activations)
    near_cots = gather_z(after(out_cotangent, near))
    acts, cots = gather_x(near), gather_x(near_cots)

    pair = chip_sum(to_hidden(table, acts, in_tiles, True))
    other = swap_z(pair)
    gate = gated(pair, other)
    gate = *gate, *swap_core(gate)
    out_parts = to_features(table, gate, out_tiles, True)

    back_pair = chip_sum(to_hidden(table, cots, out_tiles, False, out_parts[:1]))
    out_grad = to_out_tiles(table, cots, gate, back_pair[:1])
    grad = ungated(pair, other, back_pair, swap_z(back_pair), (out_grad,))
    grad = *grad, *swap_core(grad)
    out_total = add(*scatter_x(*out_parts)).astype(BF16)
    act_parts = to_features(table, grad, in_tiles, False)
    chunks = to_in_tiles(table, acts, grad, out_grad, act_parts[:1])
    grads = sum_dp(after(chunks, out_total))
    outs = pack(out_total, *scatter_x(*act_parts))
    out_grad, in_grad = spread_dp(table, grads)
    outs = scatter_z(*outs)
    return outs[0], outs[1], in_grad[None, None], out_grad[None, None]


def solution(mesh):
    in_specs = (
        P(("col", "dp"), "row"),
        P("row", "col", None, None, None),
        P("row", "col", None, None, None),
        P("row", "col", None),
        P(("col", "dp"), "row"),
    )
    out_specs = (
        P(("col", "dp"), "row"),
        P(("col", "dp"), "row"),
        P("row", "col", None, None, None),
        P("row", "col", None, None, None),
    )
    return jax.shard_map(
        per_device, mesh=mesh, in_specs=in_specs, out_specs=out_specs, check_vma=False
    )
```

```python
import functools

import jax
import jax.numpy as jnp
import numpy as np
from jax import lax
from jax.experimental import pallas as pl
from jax.experimental.pallas import tpu as pltpu
from jax.sharding import PartitionSpec as P

BLK = 256
CAP = 8
D_BLOCKS = 12
F_BLOCKS = 6
ROWS = 384
GROUP = 96
HALF = 48
PART = 24
WIDE = D_BLOCKS * BLK
HIDDEN = F_BLOCKS * BLK
F32 = jnp.float32
BF16 = jnp.bfloat16

VMEM = pl.BlockSpec(memory_space=pltpu.VMEM)
SMEM = pl.BlockSpec(memory_space=pltpu.SMEM)
ANY = pl.BlockSpec(memory_space=pl.ANY)
LIMIT = 48 * 1024 * 1024


def swap_core(halves):
    return [lax.ppermute(v, "row", [(i, i ^ 1) for i in range(4)]) for v in halves]


def swap_z(v):
    return lax.ppermute(v, "row", [(i, i ^ 2) for i in range(4)])


def x_to(v, k):
    return lax.ppermute(v, "col", [(i, i // 4 * 4 + (i + k) % 4) for i in range(16)])


def z_to(v, k):
    return lax.ppermute(v, "col", [(i, (i + 4 * k) % 16) for i in range(16)])


def y_to(v, k):
    return lax.ppermute(v, "dp", [(i, (i + k) % 4) for i in range(4)])


def y_swap(v, k):
    return lax.ppermute(v, "dp", [(i, i ^ k) for i in range(4)])


def add(*terms):
    return functools.reduce(jnp.add, [t.astype(F32) for t in terms])


def gather_z(v):
    before, after, across = z_to(v, 1), z_to(v, -1), z_to(v, 2)
    return jnp.concatenate([v, before, after, across], axis=0)


def gather_x(own):
    left, right = x_to(own, 1), x_to(own, -1)
    return own, left, right, x_to(left[:HALF], 1), x_to(right[HALF:], -1)


def scatter_x(own, left, right, across_a, across_b):
    to_left, to_right = relay(left, right, x_to(across_a, 1), x_to(across_b, -1))
    return (own, x_to(to_right, 1), x_to(to_left, -1)), to_left


def scatter_z(own, before, after, out_across, act_across):
    before, after = pass_on(before, after, z_to(out_across, -1), z_to(act_across, 1))
    return own, z_to(before, -1), z_to(after, 1)


def sum_dp(chunks):
    return add(*(y_to(c, k) if k else c for k, c in enumerate(chunks))).astype(BF16)


def halve_dp(keep, send):
    both = add(keep, y_swap(send, 1)).astype(BF16)
    return add(both[:2], y_swap(both[2:], 2)).astype(BF16)


def spread_dp(table, total):
    before, after = y_to(total, 1), y_to(total, -1)
    return in_order(table, (total, before, after, y_to(before[:2], 1), y_to(after[2:], -1)))


def dot(a, b, contract):
    return lax.dot_general(a, b, (contract, ((), ())), preferred_element_type=F32)


def pick(windows, block):
    at = pl.ds(pl.multiple_of(block * BLK, BLK), BLK)
    return jnp.concatenate([ref[first : first + rows, at] for ref, first, rows in windows], axis=0)


def call(body, outs, scratch, ins, after=(), table=True):
    def run(*refs):
        body(*refs[: len(ins)], *refs[len(ins) + len(after) :])

    return pl.pallas_call(
        run,
        out_shape=[jax.ShapeDtypeStruct(s, BF16) for s in outs],
        in_specs=[SMEM] * table + [VMEM] * (len(ins) - table) + [ANY] * len(after),
        out_specs=[VMEM] * len(outs),
        scratch_shapes=scratch,
        compiler_params=pltpu.CompilerParams(vmem_limit_bytes=LIMIT),
        cost_estimate=pl.CostEstimate(flops=0, bytes_accessed=0, transcendentals=0),
    )(*ins, *after)


def windows(refs):
    return [(ref, 0, ref.shape[0]) for ref in refs]


def quarter(table_ref, i):
    return pl.ds(pl.multiple_of((table_ref[CAP + 1] * 2 + i) % 4 * GROUP, GROUP), GROUP)


def to_hidden(table, panel, tiles, features_first, after=(), one=False):
    n = len(panel)

    def body(table_ref, *refs):
        rows, tiles_ref, out_refs, acc = windows(refs[:n]), refs[n], refs[n + 1 : -1], refs[-1]
        acc[...] = jnp.zeros_like(acc)
        for s in range(CAP):
            code = table_ref[s]

            @pl.when(code >= 0)
            def _():
                x = pick(rows, code // F_BLOCKS)
                at = pl.ds(pl.multiple_of(code % F_BLOCKS * BLK, BLK), BLK)
                acc[:, at] += dot(x, tiles_ref[s], ((1,), (0 if features_first else 1,)))

        for i in range(4):
            part = acc[quarter(table_ref, i), :].astype(BF16)
            if i < 2 or not one:
                out_refs[i][...] = part
            else:
                out_refs[2][(i - 2) * GROUP : (i - 1) * GROUP, :] = part

    return call(
        body, [(GROUP, HIDDEN)] * 2 + ([(ROWS // 2, HIDDEN)] if one else [(GROUP, HIDDEN)] * 2), [pltpu.VMEM((ROWS, HIDDEN), F32)], (table, *panel, tiles), after
    )


PANEL = pltpu.VMEM((ROWS, HIDDEN), BF16)


def fill_panel(panel, table_ref, quarters):
    for i, ref in enumerate(quarters):
        panel[quarter(table_ref, i), :] = ref[...]


def features(table_ref, quarters, tiles_ref, panel, acc, hidden_first):
    fill_panel(panel, table_ref, quarters)
    acc[...] = jnp.zeros_like(acc)
    for s in range(CAP):
        code = table_ref[s]

        @pl.when(code >= 0)
        def _():
            x = pick([(panel, 0, ROWS)], code % F_BLOCKS)
            at = pl.ds(pl.multiple_of(code // F_BLOCKS * BLK, BLK), BLK)
            acc[:, at] += dot(x, tiles_ref[s], ((1,), (0 if hidden_first else 1,)))


ACROSS = (GROUP, GROUP, GROUP, HALF, HALF)


def to_features(table, quarters, tiles, hidden_first, rows=ACROSS, after=()):
    def body(table_ref, *refs):
        out_refs, panel, acc = refs[5:-2], refs[-2], refs[-1]
        features(table_ref, refs[:4], refs[4], panel, acc, hidden_first)
        first = 0
        for ref, n in zip(out_refs, rows):
            ref[...] = acc[first : first + n, :].astype(BF16)
            first += n

    return call(
        body, [(n, WIDE) for n in rows], [PANEL, pltpu.VMEM((ROWS, WIDE), F32)],
        (table, *quarters, tiles), after,
    )


def relay(left, right, from_left, from_right):
    def body(left_ref, right_ref, from_left_ref, from_right_ref, to_left, to_right):
        to_right[:HALF, :] = add(right_ref[:HALF, :], from_left_ref[...]).astype(BF16)
        to_right[HALF:, :] = right_ref[HALF:, :]
        to_left[:HALF, :] = left_ref[:HALF, :]
        to_left[HALF:, :] = add(left_ref[HALF:, :], from_right_ref[...]).astype(BF16)

    return call(body, [(GROUP, WIDE)] * 2, [], (left, right, from_left, from_right), (), False)


def pack(out_total, *terms):
    def body(out_ref, t0, t1, t2, *packed):
        out = out_ref[...].astype(F32)
        act = add(t0[...], t1[...], t2[...])
        for i, ref in enumerate(packed[:3]):
            ref[0] = out[i * PART : (i + 1) * PART].astype(BF16)
            ref[1] = act[i * PART : (i + 1) * PART].astype(BF16)
        packed[3][...] = out[3 * PART :].astype(BF16)
        packed[4][...] = act[3 * PART :].astype(BF16)

    outs = [(2, PART, WIDE)] * 3 + [(PART, WIDE)] * 2
    return call(body, outs, [], (out_total, *terms), (), False)


def pass_on(before, after, out_term, act_term):
    def body(before_ref, after_ref, out_ref, act_ref, before_out, after_out):
        before_out[0] = add(before_ref[0], out_ref[...]).astype(BF16)
        before_out[1] = before_ref[1]
        after_out[0] = after_ref[0]
        after_out[1] = add(after_ref[1], act_ref[...]).astype(BF16)

    return call(body, [(2, PART, WIDE)] * 2, [], (before, after, out_term, act_term), (), False)


def tile(table_ref, s, rows, panel_ref, features_first, put):
    code = table_ref[s]

    @pl.when(code >= 0)
    def _():
        x = pick(rows, code // F_BLOCKS)
        h = pick([(panel_ref, 0, ROWS)], code % F_BLOCKS)
        pair = (x, h) if features_first else (h, x)
        put(dot(*pair, ((0,), (0,))).astype(BF16))

    @pl.when(code < 0)
    def _():
        put(jnp.zeros((BLK, BLK), BF16))


def to_out_tiles(table, panel, quarters, after):
    n = len(panel)

    def body(table_ref, *refs):
        keep, send, panel_ref = refs[-3:]
        fill_panel(panel_ref, table_ref, refs[n : n + 4])
        y = table_ref[CAP]
        near = y + 1 - y % 2 * 2
        for ref, at, chunk in ((keep, 0, y), (keep, 2, (y + 2) % 4), (send, 0, near), (send, 2, (near + 2) % 4)):
            for j in range(2):
                put = functools.partial(ref.__setitem__, at + j)
                tile(table_ref, chunk * 2 + j, windows(refs[:n]), panel_ref, False, put)

    return call(body, [(4, BLK, BLK)] * 2, [PANEL], (table, *panel, *quarters), after)


def to_in_tiles(table, panel, quarters, after):
    n = len(panel)

    def body(table_ref, *refs):
        chunks, panel_ref = refs[n + 4 : -1], refs[-1]
        fill_panel(panel_ref, table_ref, refs[n : n + 4])
        for k, ref in enumerate(chunks):
            for j in range(2):
                put = functools.partial(ref.__setitem__, j)
                tile(table_ref, (table_ref[CAP] + k) % 4 * 2 + j, windows(refs[:n]), panel_ref, True, put)

    return call(body, [(2, BLK, BLK)] * 4, [PANEL], (table, *panel, *quarters), after)


def in_order(table, parts):
    def body(table_ref, own, before, after, across_out, across_in, out_grad, in_grad):
        def at(k):
            return pl.ds((table_ref[CAP] + k) % 4 * 2, 2)

        for k, ref in ((0, own), (3, before), (1, after)):
            out_grad[at(k)] = ref[:2]
            in_grad[at(k)] = ref[2:]
        out_grad[at(2)] = across_out[...]
        in_grad[at(2)] = across_in[...]

    return call(body, [(CAP, BLK, BLK)] * 2, [], (table, *parts))


A = (2.0 / np.pi) ** 0.5
B = 0.044715


def gated(pair, other, after=()):
    def body(pair_ref, other_ref, *out_refs):
        v = add(pair_ref[...], other_ref[...])
        gate = (0.5 * v * (1.0 + jnp.tanh(A * (v + B * v * v * v)))).astype(BF16)
        for i, ref in enumerate(out_refs):
            ref[...] = gate[i * GROUP : (i + 1) * GROUP]

    return call(body, [(GROUP, HIDDEN)] * 2, [], (pair, other), after, False)


def ungated(pair, other, back_pair, back_other, after):
    def body(pair_ref, other_ref, back_ref, back_other_ref, *out_refs):
        v, g = add(pair_ref[...], other_ref[...]), add(back_ref[...], back_other_ref[...])
        t = jnp.tanh(A * (v + B * v * v * v))
        slope = 0.5 * (1.0 + t) + 0.5 * v * (1.0 - t * t) * (A * (1.0 + 3.0 * B * v * v))
        grad = (g * slope).astype(BF16)
        for i, ref in enumerate(out_refs):
            ref[...] = grad[i * GROUP : (i + 1) * GROUP]

    return call(body, [(GROUP, HIDDEN)] * 2, [], (pair, other, back_pair, back_other), after, False)


def chip_sum(quarters):
    arrived = swap_core(quarters[2:])
    kept = jnp.concatenate(quarters[:2], axis=0)
    return add(kept, jnp.concatenate(arrived, axis=0)).astype(BF16)


def after(value, *others):
    return lax.optimization_barrier((value, others))[0]


def per_device(activations, in_tiles, out_tiles, block_slots, out_cotangent):
    places = jnp.stack([lax.axis_index("dp"), lax.axis_index("row") % 2]).astype(jnp.int32)
    table = jnp.concatenate([block_slots[0, 0], places])
    in_tiles, out_tiles = in_tiles[0, 0], out_tiles[0, 0]

    near = gather_z(activations)
    near_cots = gather_z(after(out_cotangent, near))
    acts, cots = gather_x(near), gather_x(near_cots)

    pair = chip_sum(to_hidden(table, acts, in_tiles, True, one=False))
    other = swap_z(pair)
    gate = gated(pair, other)
    gate = *gate, *swap_core(gate)
    out_parts = to_features(table, gate, out_tiles, True)
    back_pair = chip_sum(to_hidden(table, cots, out_tiles, False, out_parts[:1], one=True))
    out_grad = to_out_tiles(table, cots, gate, (back_pair,))
    grad = ungated(pair, other, back_pair, swap_z(back_pair), out_grad[:1])
    grad = *grad, *swap_core(grad)
    out_total = add(*scatter_x(*out_parts)[0]).astype(BF16)
    act_parts = to_features(table, grad, in_tiles, False)
    chunks = to_in_tiles(table, acts, grad, act_parts[:1])
    act_terms, sent = scatter_x(*act_parts)
    out_sum = halve_dp(*out_grad)
    in_sum = sum_dp(after(chunks, sent, out_total, out_sum))
    grads = jnp.concatenate([out_sum, in_sum], axis=0)
    outs = scatter_z(*pack(out_total, *act_terms))
    out_grad, in_grad = spread_dp(table, grads)
    outs = add(*after(outs, out_grad)).astype(BF16)
    return outs[0], outs[1], in_grad[None, None], out_grad[None, None]


def solution(mesh):
    in_specs = (
        P(("col", "dp"), "row"),
        P("row", "col", None, None, None),
        P("row", "col", None, None, None),
        P("row", "col", None),
        P(("col", "dp"), "row"),
    )
    out_specs = (
        P(("col", "dp"), "row"),
        P(("col", "dp"), "row"),
        P("row", "col", None, None, None),
        P("row", "col", None, None, None),
    )
    return jax.shard_map(
        per_device, mesh=mesh, in_specs=in_specs, out_specs=out_specs, check_vma=False
    )
```

```python
import functools

import jax
import jax.numpy as jnp
import numpy as np
from jax import lax
from jax.experimental import pallas as pl
from jax.experimental.pallas import tpu as pltpu
from jax.sharding import PartitionSpec as P

BLK = 256
CAP = 8
D_BLOCKS = 12
F_BLOCKS = 6
ROWS = 384
GROUP = 96
HALF = 48
PART = 24
WIDE = D_BLOCKS * BLK
HIDDEN = F_BLOCKS * BLK
F32 = jnp.float32
BF16 = jnp.bfloat16

VMEM = pl.BlockSpec(memory_space=pltpu.VMEM)
SMEM = pl.BlockSpec(memory_space=pltpu.SMEM)
ANY = pl.BlockSpec(memory_space=pl.ANY)
LIMIT = 48 * 1024 * 1024


def swap_core(halves):
    return [lax.ppermute(v, "row", [(i, i ^ 1) for i in range(4)]) for v in halves]


def swap_z(v):
    return lax.ppermute(v, "row", [(i, i ^ 2) for i in range(4)])


def x_to(v, k):
    return lax.ppermute(v, "col", [(i, i // 4 * 4 + (i + k) % 4) for i in range(16)])


def z_to(v, k):
    return lax.ppermute(v, "col", [(i, (i + 4 * k) % 16) for i in range(16)])


def y_to(v, k):
    return lax.ppermute(v, "dp", [(i, (i + k) % 4) for i in range(4)])


def y_swap(v, k):
    return lax.ppermute(v, "dp", [(i, i ^ k) for i in range(4)])


def add(*terms):
    return functools.reduce(jnp.add, [t.astype(F32) for t in terms])


def gather_z(v):
    before, after, across = z_to(v, 1), z_to(v, -1), z_to(v, 2)
    return jnp.concatenate([v, before, after, across], axis=0)


def gather_x(own):
    left, right = x_to(own, 1), x_to(own, -1)
    return own, left, right, x_to(left[:HALF], 1), x_to(right[HALF:], -1)


def scatter_x(own, left, right, across_a, across_b, later=()):
    to_left, to_right = relay(left, right, x_to(across_a, 1), x_to(across_b, -1), later)
    return (own, x_to(to_right, 1), x_to(to_left, -1)), to_left


def scatter_z(own, before, after, out_across, act_across):
    before, after = pass_on(before, after, z_to(out_across, -1), z_to(act_across, 1))
    return own, z_to(before, -1), z_to(after, 1)


def sum_dp(chunks):
    return add(*(y_to(c, k) if k else c for k, c in enumerate(chunks))).astype(BF16)


def halve_dp(keep, send, later):
    both = after(add(keep, y_swap(send, 1)).astype(BF16), later)
    return add(both[:2], y_swap(both[2:], 2)).astype(BF16)


def spread_dp(table, total):
    before, after = y_to(total, 1), y_to(total, -1)
    return in_order(table, (total, before, after, y_to(before[:2], 1), y_to(after[2:], -1)))


def dot(a, b, contract):
    return lax.dot_general(a, b, (contract, ((), ())), preferred_element_type=F32)


def pick(windows, block):
    at = pl.ds(pl.multiple_of(block * BLK, BLK), BLK)
    return jnp.concatenate([ref[first : first + rows, at] for ref, first, rows in windows], axis=0)


def call(body, outs, scratch, ins, after=(), table=True):
    def run(*refs):
        body(*refs[: len(ins)], *refs[len(ins) + len(after) :])

    return pl.pallas_call(
        run,
        out_shape=[jax.ShapeDtypeStruct(s, BF16) for s in outs],
        in_specs=[SMEM] * table + [VMEM] * (len(ins) - table) + [ANY] * len(after),
        out_specs=[VMEM] * len(outs),
        scratch_shapes=scratch,
        compiler_params=pltpu.CompilerParams(vmem_limit_bytes=LIMIT),
        cost_estimate=pl.CostEstimate(flops=0, bytes_accessed=0, transcendentals=0),
    )(*ins, *after)


def windows(refs):
    return [(ref, 0, ref.shape[0]) for ref in refs]


def quarter(table_ref, i):
    return pl.ds(pl.multiple_of((table_ref[CAP + 1] * 2 + i) % 4 * GROUP, GROUP), GROUP)


def to_hidden(table, panel, tiles, features_first, after=(), one=False):
    n = len(panel)

    def body(table_ref, *refs):
        rows, tiles_ref, out_refs, acc = windows(refs[:n]), refs[n], refs[n + 1 : -1], refs[-1]
        acc[...] = jnp.zeros_like(acc)
        for s in range(CAP):
            code = table_ref[s]

            @pl.when(code >= 0)
            def _():
                x = pick(rows, code // F_BLOCKS)
                at = pl.ds(pl.multiple_of(code % F_BLOCKS * BLK, BLK), BLK)
                acc[:, at] += dot(x, tiles_ref[s], ((1,), (0 if features_first else 1,)))

        for i in range(4):
            part = acc[quarter(table_ref, i), :].astype(BF16)
            if i < 2 or not one:
                out_refs[i][...] = part
            else:
                out_refs[2][(i - 2) * GROUP : (i - 1) * GROUP, :] = part

    return call(
        body, [(GROUP, HIDDEN)] * 2 + ([(ROWS // 2, HIDDEN)] if one else [(GROUP, HIDDEN)] * 2), [pltpu.VMEM((ROWS, HIDDEN), F32)], (table, *panel, tiles), after
    )


PANEL = pltpu.VMEM((ROWS, HIDDEN), BF16)


def fill_panel(panel, table_ref, quarters):
    for i, ref in enumerate(quarters):
        panel[quarter(table_ref, i), :] = ref[...]


def features(table_ref, quarters, tiles_ref, panel, acc, hidden_first):
    fill_panel(panel, table_ref, quarters)
    acc[...] = jnp.zeros_like(acc)
    for s in range(CAP):
        code = table_ref[s]

        @pl.when(code >= 0)
        def _():
            x = pick([(panel, 0, ROWS)], code % F_BLOCKS)
            at = pl.ds(pl.multiple_of(code // F_BLOCKS * BLK, BLK), BLK)
            acc[:, at] += dot(x, tiles_ref[s], ((1,), (0 if hidden_first else 1,)))


ACROSS = (GROUP, GROUP, GROUP, HALF, HALF)


def to_features(table, quarters, tiles, hidden_first, rows=ACROSS, after=()):
    def body(table_ref, *refs):
        out_refs, panel, acc = refs[5:-2], refs[-2], refs[-1]
        features(table_ref, refs[:4], refs[4], panel, acc, hidden_first)
        first = 0
        for ref, n in zip(out_refs, rows):
            ref[...] = acc[first : first + n, :].astype(BF16)
            first += n

    return call(
        body, [(n, WIDE) for n in rows], [PANEL, pltpu.VMEM((ROWS, WIDE), F32)],
        (table, *quarters, tiles), after,
    )


def relay(left, right, from_left, from_right, after=()):
    def body(left_ref, right_ref, from_left_ref, from_right_ref, to_left, to_right):
        to_right[:HALF, :] = add(right_ref[:HALF, :], from_left_ref[...]).astype(BF16)
        to_right[HALF:, :] = right_ref[HALF:, :]
        to_left[:HALF, :] = left_ref[:HALF, :]
        to_left[HALF:, :] = add(left_ref[HALF:, :], from_right_ref[...]).astype(BF16)

    return call(body, [(GROUP, WIDE)] * 2, [], (left, right, from_left, from_right), after, False)


def pack(out_total, *terms):
    def body(out_ref, t0, t1, t2, *packed):
        out = out_ref[...].astype(F32)
        act = add(t0[...], t1[...], t2[...])
        for i, ref in enumerate(packed[:3]):
            ref[0] = out[i * PART : (i + 1) * PART].astype(BF16)
            ref[1] = act[i * PART : (i + 1) * PART].astype(BF16)
        packed[3][...] = out[3 * PART :].astype(BF16)
        packed[4][...] = act[3 * PART :].astype(BF16)

    outs = [(2, PART, WIDE)] * 3 + [(PART, WIDE)] * 2
    return call(body, outs, [], (out_total, *terms), (), False)


def pass_on(before, after, out_term, act_term):
    def body(before_ref, after_ref, out_ref, act_ref, before_out, after_out):
        before_out[0] = add(before_ref[0], out_ref[...]).astype(BF16)
        before_out[1] = before_ref[1]
        after_out[0] = after_ref[0]
        after_out[1] = add(after_ref[1], act_ref[...]).astype(BF16)

    return call(body, [(2, PART, WIDE)] * 2, [], (before, after, out_term, act_term), (), False)


def tile(table_ref, s, rows, panel_ref, features_first, put):
    code = table_ref[s]

    @pl.when(code >= 0)
    def _():
        x = pick(rows, code // F_BLOCKS)
        h = pick([(panel_ref, 0, ROWS)], code % F_BLOCKS)
        pair = (x, h) if features_first else (h, x)
        put(dot(*pair, ((0,), (0,))).astype(BF16))

    @pl.when(code < 0)
    def _():
        put(jnp.zeros((BLK, BLK), BF16))


def to_out_tiles(table, panel, quarters, after):
    n = len(panel)

    def body(table_ref, *refs):
        keep, send, panel_ref = refs[-3:]
        fill_panel(panel_ref, table_ref, refs[n : n + 4])
        y = table_ref[CAP]
        near = y + 1 - y % 2 * 2
        for ref, at, chunk in ((keep, 0, y), (keep, 2, (y + 2) % 4), (send, 0, near), (send, 2, (near + 2) % 4)):
            for j in range(2):
                put = functools.partial(ref.__setitem__, at + j)
                tile(table_ref, chunk * 2 + j, windows(refs[:n]), panel_ref, False, put)

    return call(body, [(4, BLK, BLK)] * 2, [PANEL], (table, *panel, *quarters), after)


def to_in_tiles(table, panel, quarters, after):
    n = len(panel)

    def body(table_ref, *refs):
        chunks, panel_ref = refs[n + 4 : -1], refs[-1]
        fill_panel(panel_ref, table_ref, refs[n : n + 4])
        for k, ref in enumerate(chunks):
            for j in range(2):
                put = functools.partial(ref.__setitem__, j)
                tile(table_ref, (table_ref[CAP] + k) % 4 * 2 + j, windows(refs[:n]), panel_ref, True, put)

    return call(body, [(2, BLK, BLK)] * 4, [PANEL], (table, *panel, *quarters), after)


def in_order(table, parts):
    def body(table_ref, own, before, after, across_out, across_in, out_grad, in_grad):
        def at(k):
            return pl.ds((table_ref[CAP] + k) % 4 * 2, 2)

        for k, ref in ((0, own), (3, before), (1, after)):
            out_grad[at(k)] = ref[:2]
            in_grad[at(k)] = ref[2:]
        out_grad[at(2)] = across_out[...]
        in_grad[at(2)] = across_in[...]

    return call(body, [(CAP, BLK, BLK)] * 2, [], (table, *parts))


A = (2.0 / np.pi) ** 0.5
B = 0.044715


def gated(pair, other, after=()):
    def body(pair_ref, other_ref, *out_refs):
        v = add(pair_ref[...], other_ref[...])
        gate = (0.5 * v * (1.0 + jnp.tanh(A * (v + B * v * v * v)))).astype(BF16)
        for i, ref in enumerate(out_refs):
            ref[...] = gate[i * GROUP : (i + 1) * GROUP]

    return call(body, [(GROUP, HIDDEN)] * 2, [], (pair, other), after, False)


def ungated(pair, other, back_pair, back_other, after):
    def body(pair_ref, other_ref, back_ref, back_other_ref, *out_refs):
        v, g = add(pair_ref[...], other_ref[...]), add(back_ref[...], back_other_ref[...])
        t = jnp.tanh(A * (v + B * v * v * v))
        slope = 0.5 * (1.0 + t) + 0.5 * v * (1.0 - t * t) * (A * (1.0 + 3.0 * B * v * v))
        grad = (g * slope).astype(BF16)
        for i, ref in enumerate(out_refs):
            ref[...] = grad[i * GROUP : (i + 1) * GROUP]

    return call(body, [(GROUP, HIDDEN)] * 2, [], (pair, other, back_pair, back_other), after, False)


def chip_sum(quarters):
    arrived = swap_core(quarters[2:])
    kept = jnp.concatenate(quarters[:2], axis=0)
    return add(kept, jnp.concatenate(arrived, axis=0)).astype(BF16)


def after(value, *others):
    return lax.optimization_barrier((value, others))[0]


def per_device(activations, in_tiles, out_tiles, block_slots, out_cotangent):
    places = jnp.stack([lax.axis_index("dp"), lax.axis_index("row") % 2]).astype(jnp.int32)
    table = jnp.concatenate([block_slots[0, 0], places])
    in_tiles, out_tiles = in_tiles[0, 0], out_tiles[0, 0]

    near = gather_z(activations)
    near_cots = gather_z(after(out_cotangent, near))
    acts, cots = gather_x(near), gather_x(near_cots)

    pair = chip_sum(to_hidden(table, acts, in_tiles, True, one=False))
    other = swap_z(pair)
    gate = gated(pair, other)
    gate = *gate, *swap_core(gate)
    out_parts = to_features(table, gate, out_tiles, True)
    back_pair = chip_sum(to_hidden(table, cots, out_tiles, False, out_parts[:1], one=True))
    out_grad = to_out_tiles(table, cots, gate, (back_pair,))
    grad = ungated(pair, other, back_pair, swap_z(back_pair), out_grad[:1])
    grad = *grad, *swap_core(grad)
    out_total = add(*scatter_x(*out_parts)[0]).astype(BF16)
    act_parts = to_features(table, grad, in_tiles, False)
    chunks = to_in_tiles(table, acts, grad, act_parts[:1])
    act_terms, sent = scatter_x(*act_parts, chunks[:1])
    out_sum = halve_dp(*out_grad, act_parts[0])
    in_sum = sum_dp(after(chunks, sent, out_total))
    grads = jnp.concatenate([out_sum, in_sum], axis=0)
    outs = scatter_z(*pack(out_total, *act_terms))
    out_grad, in_grad = spread_dp(table, grads)
    outs = add(*after(outs, out_grad)).astype(BF16)
    return outs[0], outs[1], in_grad[None, None], out_grad[None, None]


def solution(mesh):
    in_specs = (
        P(("col", "dp"), "row"),
        P("row", "col", None, None, None),
        P("row", "col", None, None, None),
        P("row", "col", None),
        P(("col", "dp"), "row"),
    )
    out_specs = (
        P(("col", "dp"), "row"),
        P(("col", "dp"), "row"),
        P("row", "col", None, None, None),
        P("row", "col", None, None, None),
    )
    return jax.shard_map(
        per_device, mesh=mesh, in_specs=in_specs, out_specs=out_specs, check_vma=False
    )
```

```python
import functools

import jax
import jax.numpy as jnp
import numpy as np
from jax import lax
from jax.experimental import pallas as pl
from jax.experimental.pallas import tpu as pltpu
from jax.sharding import PartitionSpec as P

BLK = 256
CAP = 8
D_BLOCKS = 12
F_BLOCKS = 6
ROWS = 384
GROUP = 96
HALF = 48
PART = 24
WIDE = D_BLOCKS * BLK
HIDDEN = F_BLOCKS * BLK
F32 = jnp.float32
BF16 = jnp.bfloat16

VMEM = pl.BlockSpec(memory_space=pltpu.VMEM)
SMEM = pl.BlockSpec(memory_space=pltpu.SMEM)
ANY = pl.BlockSpec(memory_space=pl.ANY)
LIMIT = 48 * 1024 * 1024


def swap_core(halves):
    return [lax.ppermute(v, "row", [(i, i ^ 1) for i in range(4)]) for v in halves]


def swap_z(v):
    return lax.ppermute(v, "row", [(i, i ^ 2) for i in range(4)])


def x_to(v, k):
    return lax.ppermute(v, "col", [(i, i // 4 * 4 + (i + k) % 4) for i in range(16)])


def z_to(v, k):
    return lax.ppermute(v, "col", [(i, (i + 4 * k) % 16) for i in range(16)])


def y_to(v, k):
    return lax.ppermute(v, "dp", [(i, (i + k) % 4) for i in range(4)])


def y_swap(v, k):
    return lax.ppermute(v, "dp", [(i, i ^ k) for i in range(4)])


def add(*terms):
    return functools.reduce(jnp.add, [t.astype(F32) for t in terms])


def gather_z(v):
    before, after, across = z_to(v, 1), z_to(v, -1), z_to(v, 2)
    return jnp.concatenate([v, before, after, across], axis=0)


def gather_x(own):
    left, right = x_to(own, 1), x_to(own, -1)
    return own, left, right, x_to(left[:HALF], 1), x_to(right[HALF:], -1)


def scatter_x(own, left, right, across_a, across_b, later=()):
    to_left, to_right = relay(left, right, x_to(across_a, 1), x_to(across_b, -1), later)
    return (own, x_to(to_right, 1), x_to(to_left, -1)), to_left


def scatter_z(own, before, after, out_across, act_across):
    before, after = pass_on(before, after, z_to(out_across, -1), z_to(act_across, 1))
    return own, z_to(before, -1), z_to(after, 1)


def sum_dp(chunks):
    return add(*(y_to(c, k) if k else c for k, c in enumerate(chunks))).astype(BF16)


def halve_dp(keep, send, later):
    both = after(add(keep, y_swap(send, 1)).astype(BF16), later)
    return add(both[:2], y_swap(both[2:], 2)).astype(BF16)


def spread_dp(table, total):
    before, after = y_to(total, 1), y_to(total, -1)
    return in_order(table, (total, before, after, y_to(before[:2], 1), y_to(after[2:], -1)))


def dot(a, b, contract):
    return lax.dot_general(a, b, (contract, ((), ())), preferred_element_type=F32)


def pick(windows, block):
    at = pl.ds(pl.multiple_of(block * BLK, BLK), BLK)
    return jnp.concatenate([ref[first : first + rows, at] for ref, first, rows in windows], axis=0)


def call(body, outs, scratch, ins, after=(), table=True):
    def run(*refs):
        body(*refs[: len(ins)], *refs[len(ins) + len(after) :])

    return pl.pallas_call(
        run,
        out_shape=[jax.ShapeDtypeStruct(s, BF16) for s in outs],
        in_specs=[SMEM] * table + [VMEM] * (len(ins) - table) + [ANY] * len(after),
        out_specs=[VMEM] * len(outs),
        scratch_shapes=scratch,
        compiler_params=pltpu.CompilerParams(vmem_limit_bytes=LIMIT),
        cost_estimate=pl.CostEstimate(flops=0, bytes_accessed=0, transcendentals=0),
    )(*ins, *after)


def windows(refs):
    return [(ref, 0, ref.shape[0]) for ref in refs]


def quarter(table_ref, i):
    return pl.ds(pl.multiple_of((table_ref[CAP + 1] * 2 + i) % 4 * GROUP, GROUP), GROUP)


def accumulate(out_refs, at, product):
    first = 0
    for ref in out_refs:
        rows = ref.shape[0]
        ref[:, at] = (ref[:, at].astype(F32) + product[first : first + rows]).astype(BF16)
        first += rows


def to_hidden(table, panel, tiles, features_first, after=(), one=False):
    n = len(panel)

    def body(table_ref, *refs):
        rows, tiles_ref, out_refs = windows(refs[:n]), refs[n], refs[n + 1 :]
        first_core = table_ref[CAP + 1] == 0
        for ref in out_refs:
            ref[...] = jnp.zeros_like(ref)
        for s in range(CAP):
            code = table_ref[s]

            @pl.when(code >= 0)
            def _():
                x = pick(rows, code // F_BLOCKS)
                other = jnp.concatenate([x[ROWS // 2 :], x[: ROWS // 2]], axis=0)
                x = lax.select(first_core, x, other)
                at = pl.ds(pl.multiple_of(code % F_BLOCKS * BLK, BLK), BLK)
                accumulate(out_refs, at, dot(x, tiles_ref[s], ((1,), (0 if features_first else 1,))))

    sent = [(ROWS // 2, HIDDEN)] if one else [(GROUP, HIDDEN)] * 2
    return call(body, [(GROUP, HIDDEN)] * 2 + sent, [], (table, *panel, tiles), after)


PANEL = pltpu.VMEM((ROWS, HIDDEN), BF16)


def fill_panel(panel, table_ref, quarters):
    for i, ref in enumerate(quarters):
        panel[quarter(table_ref, i), :] = ref[...]


ACROSS = (GROUP, GROUP, GROUP, HALF, HALF)


def to_features(table, quarters, tiles, hidden_first, rows=ACROSS, after=()):
    def body(table_ref, *refs):
        tiles_ref, out_refs, panel = refs[4], refs[5:-1], refs[-1]
        fill_panel(panel, table_ref, refs[:4])
        for ref in out_refs:
            ref[...] = jnp.zeros_like(ref)
        for s in range(CAP):
            code = table_ref[s]

            @pl.when(code >= 0)
            def _():
                x = pick([(panel, 0, ROWS)], code % F_BLOCKS)
                at = pl.ds(pl.multiple_of(code // F_BLOCKS * BLK, BLK), BLK)
                accumulate(out_refs, at, dot(x, tiles_ref[s], ((1,), (0 if hidden_first else 1,))))

    return call(body, [(n, WIDE) for n in rows], [PANEL], (table, *quarters, tiles), after)


def relay(left, right, from_left, from_right, after=()):
    def body(left_ref, right_ref, from_left_ref, from_right_ref, to_left, to_right):
        to_right[:HALF, :] = add(right_ref[:HALF, :], from_left_ref[...]).astype(BF16)
        to_right[HALF:, :] = right_ref[HALF:, :]
        to_left[:HALF, :] = left_ref[:HALF, :]
        to_left[HALF:, :] = add(left_ref[HALF:, :], from_right_ref[...]).astype(BF16)

    return call(body, [(GROUP, WIDE)] * 2, [], (left, right, from_left, from_right), after, False)


def pack(out_total, *terms):
    def body(out_ref, t0, t1, t2, *packed):
        out = out_ref[...].astype(F32)
        act = add(t0[...], t1[...], t2[...])
        for i, ref in enumerate(packed[:3]):
            ref[0] = out[i * PART : (i + 1) * PART].astype(BF16)
            ref[1] = act[i * PART : (i + 1) * PART].astype(BF16)
        packed[3][...] = out[3 * PART :].astype(BF16)
        packed[4][...] = act[3 * PART :].astype(BF16)

    outs = [(2, PART, WIDE)] * 3 + [(PART, WIDE)] * 2
    return call(body, outs, [], (out_total, *terms), (), False)


def pass_on(before, after, out_term, act_term):
    def body(before_ref, after_ref, out_ref, act_ref, before_out, after_out):
        before_out[0] = add(before_ref[0], out_ref[...]).astype(BF16)
        before_out[1] = before_ref[1]
        after_out[0] = after_ref[0]
        after_out[1] = add(after_ref[1], act_ref[...]).astype(BF16)

    return call(body, [(2, PART, WIDE)] * 2, [], (before, after, out_term, act_term), (), False)


def tile(table_ref, s, rows, panel_ref, features_first, put):
    code = table_ref[s]

    @pl.when(code >= 0)
    def _():
        x = pick(rows, code // F_BLOCKS)
        h = pick([(panel_ref, 0, ROWS)], code % F_BLOCKS)
        pair = (x, h) if features_first else (h, x)
        put(dot(*pair, ((0,), (0,))).astype(BF16))

    @pl.when(code < 0)
    def _():
        put(jnp.zeros((BLK, BLK), BF16))


def to_out_tiles(table, panel, quarters, after):
    n = len(panel)

    def body(table_ref, *refs):
        keep, send, panel_ref = refs[-3:]
        fill_panel(panel_ref, table_ref, refs[n : n + 4])
        y = table_ref[CAP]
        near = y + 1 - y % 2 * 2
        for ref, at, chunk in ((keep, 0, y), (keep, 2, (y + 2) % 4), (send, 0, near), (send, 2, (near + 2) % 4)):
            for j in range(2):
                put = functools.partial(ref.__setitem__, at + j)
                tile(table_ref, chunk * 2 + j, windows(refs[:n]), panel_ref, False, put)

    return call(body, [(4, BLK, BLK)] * 2, [PANEL], (table, *panel, *quarters), after)


def to_in_tiles(table, panel, quarters, after):
    n = len(panel)

    def body(table_ref, *refs):
        chunks, panel_ref = refs[n + 4 : -1], refs[-1]
        fill_panel(panel_ref, table_ref, refs[n : n + 4])
        for k, ref in enumerate(chunks):
            for j in range(2):
                put = functools.partial(ref.__setitem__, j)
                tile(table_ref, (table_ref[CAP] + k) % 4 * 2 + j, windows(refs[:n]), panel_ref, True, put)

    return call(body, [(2, BLK, BLK)] * 4, [PANEL], (table, *panel, *quarters), after)


def in_order(table, parts):
    def body(table_ref, own, before, after, across_out, across_in, out_grad, in_grad):
        def at(k):
            return pl.ds((table_ref[CAP] + k) % 4 * 2, 2)

        for k, ref in ((0, own), (3, before), (1, after)):
            out_grad[at(k)] = ref[:2]
            in_grad[at(k)] = ref[2:]
        out_grad[at(2)] = across_out[...]
        in_grad[at(2)] = across_in[...]

    return call(body, [(CAP, BLK, BLK)] * 2, [], (table, *parts))


A = (2.0 / np.pi) ** 0.5
B = 0.044715


def gated(pair, other, after=()):
    def body(pair_ref, other_ref, *out_refs):
        v = add(pair_ref[...], other_ref[...])
        gate = (0.5 * v * (1.0 + jnp.tanh(A * (v + B * v * v * v)))).astype(BF16)
        for i, ref in enumerate(out_refs):
            ref[...] = gate[i * GROUP : (i + 1) * GROUP]

    return call(body, [(GROUP, HIDDEN)] * 2, [], (pair, other), after, False)


def ungated(pair, other, back_pair, back_other, after):
    def body(pair_ref, other_ref, back_ref, back_other_ref, *out_refs):
        v, g = add(pair_ref[...], other_ref[...]), add(back_ref[...], back_other_ref[...])
        t = jnp.tanh(A * (v + B * v * v * v))
        slope = 0.5 * (1.0 + t) + 0.5 * v * (1.0 - t * t) * (A * (1.0 + 3.0 * B * v * v))
        grad = (g * slope).astype(BF16)
        for i, ref in enumerate(out_refs):
            ref[...] = grad[i * GROUP : (i + 1) * GROUP]

    return call(body, [(GROUP, HIDDEN)] * 2, [], (pair, other, back_pair, back_other), after, False)


def chip_sum(quarters):
    arrived = swap_core(quarters[2:])
    kept = jnp.concatenate(quarters[:2], axis=0)
    return add(kept, jnp.concatenate(arrived, axis=0)).astype(BF16)


def after(value, *others):
    return lax.optimization_barrier((value, others))[0]


def per_device(activations, in_tiles, out_tiles, block_slots, out_cotangent):
    places = jnp.stack([lax.axis_index("dp"), lax.axis_index("row") % 2]).astype(jnp.int32)
    table = jnp.concatenate([block_slots[0, 0], places])
    in_tiles, out_tiles = in_tiles[0, 0], out_tiles[0, 0]

    near = gather_z(activations)
    near_cots = gather_z(after(out_cotangent, near))
    acts, cots = gather_x(near), gather_x(near_cots)

    pair = chip_sum(to_hidden(table, acts, in_tiles, True, one=False))
    other = swap_z(pair)
    gate = gated(pair, other)
    gate = *gate, *swap_core(gate)
    out_parts = to_features(table, gate, out_tiles, True)
    back_pair = chip_sum(to_hidden(table, cots, out_tiles, False, out_parts[:1], one=True))
    out_grad = to_out_tiles(table, cots, gate, (back_pair,))
    grad = ungated(pair, other, back_pair, swap_z(back_pair), out_grad[:1])
    grad = *grad, *swap_core(grad)
    out_total = add(*scatter_x(*out_parts)[0]).astype(BF16)
    act_parts = to_features(table, grad, in_tiles, False)
    chunks = to_in_tiles(table, acts, grad, act_parts[:1])
    act_terms, sent = scatter_x(*act_parts, chunks[:1])
    out_sum = halve_dp(*out_grad, act_parts[0])
    in_sum = sum_dp(after(chunks, sent, out_total))
    grads = jnp.concatenate([out_sum, in_sum], axis=0)
    outs = scatter_z(*pack(out_total, *act_terms))
    out_grad, in_grad = spread_dp(table, grads)
    outs = add(*after(outs, out_grad)).astype(BF16)
    return outs[0], outs[1], in_grad[None, None], out_grad[None, None]


def solution(mesh):
    in_specs = (
        P(("col", "dp"), "row"),
        P("row", "col", None, None, None),
        P("row", "col", None, None, None),
        P("row", "col", None),
        P(("col", "dp"), "row"),
    )
    out_specs = (
        P(("col", "dp"), "row"),
        P(("col", "dp"), "row"),
        P("row", "col", None, None, None),
        P("row", "col", None, None, None),
    )
    return jax.shard_map(
        per_device, mesh=mesh, in_specs=in_specs, out_specs=out_specs, check_vma=False
    )
```

```python
import functools

import jax
import jax.numpy as jnp
import numpy as np
from jax import lax
from jax.experimental import pallas as pl
from jax.experimental.pallas import tpu as pltpu
from jax.sharding import PartitionSpec as P

BLK = 256
CAP = 8
D_BLOCKS = 12
F_BLOCKS = 6
ROWS = 384
GROUP = 96
HALF = 48
PART = 24
WIDE = D_BLOCKS * BLK
HIDDEN = F_BLOCKS * BLK
F32 = jnp.float32
BF16 = jnp.bfloat16

VMEM = pl.BlockSpec(memory_space=pltpu.VMEM)
SMEM = pl.BlockSpec(memory_space=pltpu.SMEM)
ANY = pl.BlockSpec(memory_space=pl.ANY)
LIMIT = 48 * 1024 * 1024


def swap_core(halves):
    return [lax.ppermute(v, "row", [(i, i ^ 1) for i in range(4)]) for v in halves]


def swap_z(v):
    return lax.ppermute(v, "row", [(i, i ^ 2) for i in range(4)])


def x_to(v, k):
    return lax.ppermute(v, "col", [(i, i // 4 * 4 + (i + k) % 4) for i in range(16)])


def z_to(v, k):
    return lax.ppermute(v, "col", [(i, (i + 4 * k) % 16) for i in range(16)])


def y_to(v, k):
    return lax.ppermute(v, "dp", [(i, (i + k) % 4) for i in range(4)])


def y_swap(v, k):
    return lax.ppermute(v, "dp", [(i, i ^ k) for i in range(4)])


def add(*terms):
    return functools.reduce(jnp.add, [t.astype(F32) for t in terms])


def gather_z(v):
    across, before, after = z_to(v, 2), z_to(v, 1), z_to(v, -1)
    return jnp.concatenate([v, before, after, across], axis=0)


def gather_x(own):
    left, right = x_to(own, 1), x_to(own, -1)
    return own, left, right, x_to(left[:HALF], 1), x_to(right[HALF:], -1)


def scatter_x(own, left, right, across_a, across_b, later=()):
    to_left, to_right = relay(left, right, x_to(across_a, 1), x_to(across_b, -1), later)
    return (own, x_to(to_right, 1), x_to(to_left, -1)), to_left


def scatter_z(own, before, after, out_across, act_across):
    before, after = pass_on(before, after, z_to(out_across, -1), z_to(act_across, 1))
    return own, z_to(before, -1), z_to(after, 1)


def sum_dp(chunks):
    return add(*(y_to(c, k) if k else c for k, c in enumerate(chunks))).astype(BF16)


def halve_dp(keep, send, later):
    both = after(add(keep, y_swap(send, 1)).astype(BF16), later)
    return add(both[:2], y_swap(both[2:], 2)).astype(BF16)


def spread_dp(table, total):
    before, after = y_to(total, 1), y_to(total, -1)
    return in_order(table, (total, before, after, y_to(before[:2], 1), y_to(after[2:], -1)))


def dot(a, b, contract):
    return lax.dot_general(a, b, (contract, ((), ())), preferred_element_type=F32)


def pick(windows, block):
    at = pl.ds(pl.multiple_of(block * BLK, BLK), BLK)
    return jnp.concatenate([ref[first : first + rows, at] for ref, first, rows in windows], axis=0)


def call(body, outs, scratch, ins, after=(), table=True):
    def run(*refs):
        body(*refs[: len(ins)], *refs[len(ins) + len(after) :])

    return pl.pallas_call(
        run,
        out_shape=[jax.ShapeDtypeStruct(s, BF16) for s in outs],
        in_specs=[SMEM] * table + [VMEM] * (len(ins) - table) + [ANY] * len(after),
        out_specs=[VMEM] * len(outs),
        scratch_shapes=scratch,
        compiler_params=pltpu.CompilerParams(vmem_limit_bytes=LIMIT),
        cost_estimate=pl.CostEstimate(flops=0, bytes_accessed=0, transcendentals=0),
    )(*ins, *after)


def windows(refs):
    return [(ref, 0, ref.shape[0]) for ref in refs]


def quarter(table_ref, i):
    return pl.ds(pl.multiple_of((table_ref[CAP + 1] * 2 + i) % 4 * GROUP, GROUP), GROUP)


def accumulate(out_refs, at, product):
    first = 0
    for ref in out_refs:
        rows = ref.shape[0]
        ref[:, at] = (ref[:, at].astype(F32) + product[first : first + rows]).astype(BF16)
        first += rows


def to_hidden(table, panel, tiles, features_first, after=(), one=False):
    n = len(panel)

    def body(table_ref, *refs):
        rows, tiles_ref, out_refs = windows(refs[:n]), refs[n], refs[n + 1 :]
        first_core = table_ref[CAP + 1] == 0
        for ref in out_refs:
            ref[...] = jnp.zeros_like(ref)
        for s in range(CAP):
            code = table_ref[s]

            @pl.when(code >= 0)
            def _():
                x = pick(rows, code // F_BLOCKS)
                other = jnp.concatenate([x[ROWS // 2 :], x[: ROWS // 2]], axis=0)
                x = lax.select(first_core, x, other)
                at = pl.ds(pl.multiple_of(code % F_BLOCKS * BLK, BLK), BLK)
                accumulate(out_refs, at, dot(x, tiles_ref[s], ((1,), (0 if features_first else 1,))))

    sent = [(ROWS // 2, HIDDEN)] if one else [(GROUP, HIDDEN)] * 2
    return call(body, [(GROUP, HIDDEN)] * 2 + sent, [], (table, *panel, tiles), after)


PANEL = pltpu.VMEM((ROWS, HIDDEN), BF16)


def fill_panel(panel, table_ref, quarters):
    for i, ref in enumerate(quarters):
        panel[quarter(table_ref, i), :] = ref[...]


ACROSS = (GROUP, GROUP, GROUP, HALF, HALF)


def to_features(table, quarters, tiles, hidden_first, rows=ACROSS, after=()):
    def body(table_ref, *refs):
        tiles_ref, out_refs, panel = refs[4], refs[5:-1], refs[-1]
        fill_panel(panel, table_ref, refs[:4])
        for ref in out_refs:
            ref[...] = jnp.zeros_like(ref)
        for s in range(CAP):
            code = table_ref[s]

            @pl.when(code >= 0)
            def _():
                x = pick([(panel, 0, ROWS)], code % F_BLOCKS)
                at = pl.ds(pl.multiple_of(code // F_BLOCKS * BLK, BLK), BLK)
                accumulate(out_refs, at, dot(x, tiles_ref[s], ((1,), (0 if hidden_first else 1,))))

    return call(body, [(n, WIDE) for n in rows], [PANEL], (table, *quarters, tiles), after)


def relay(left, right, from_left, from_right, after=()):
    def body(left_ref, right_ref, from_left_ref, from_right_ref, to_left, to_right):
        to_right[:HALF, :] = add(right_ref[:HALF, :], from_left_ref[...]).astype(BF16)
        to_right[HALF:, :] = right_ref[HALF:, :]
        to_left[:HALF, :] = left_ref[:HALF, :]
        to_left[HALF:, :] = add(left_ref[HALF:, :], from_right_ref[...]).astype(BF16)

    return call(body, [(GROUP, WIDE)] * 2, [], (left, right, from_left, from_right), after, False)


def pack(out_total, *terms):
    def body(out_ref, t0, t1, t2, *packed):
        out = out_ref[...].astype(F32)
        act = add(t0[...], t1[...], t2[...])
        for i, ref in enumerate(packed[:3]):
            ref[0] = out[i * PART : (i + 1) * PART].astype(BF16)
            ref[1] = act[i * PART : (i + 1) * PART].astype(BF16)
        packed[3][...] = out[3 * PART :].astype(BF16)
        packed[4][...] = act[3 * PART :].astype(BF16)

    outs = [(2, PART, WIDE)] * 3 + [(PART, WIDE)] * 2
    return call(body, outs, [], (out_total, *terms), (), False)


def pass_on(before, after, out_term, act_term):
    def body(before_ref, after_ref, out_ref, act_ref, before_out, after_out):
        before_out[0] = add(before_ref[0], out_ref[...]).astype(BF16)
        before_out[1] = before_ref[1]
        after_out[0] = after_ref[0]
        after_out[1] = add(after_ref[1], act_ref[...]).astype(BF16)

    return call(body, [(2, PART, WIDE)] * 2, [], (before, after, out_term, act_term), (), False)


def tile(table_ref, s, rows, panel_ref, features_first, put):
    code = table_ref[s]

    @pl.when(code >= 0)
    def _():
        x = pick(rows, code // F_BLOCKS)
        h = pick([(panel_ref, 0, ROWS)], code % F_BLOCKS)
        pair = (x, h) if features_first else (h, x)
        put(dot(*pair, ((0,), (0,))).astype(BF16))

    @pl.when(code < 0)
    def _():
        put(jnp.zeros((BLK, BLK), BF16))


def to_out_tiles(table, panel, quarters, after):
    n = len(panel)

    def body(table_ref, *refs):
        keep, send, panel_ref = refs[-3:]
        fill_panel(panel_ref, table_ref, refs[n : n + 4])
        y = table_ref[CAP]
        near = y + 1 - y % 2 * 2
        for ref, at, chunk in ((keep, 0, y), (keep, 2, (y + 2) % 4), (send, 0, near), (send, 2, (near + 2) % 4)):
            for j in range(2):
                put = functools.partial(ref.__setitem__, at + j)
                tile(table_ref, chunk * 2 + j, windows(refs[:n]), panel_ref, False, put)

    return call(body, [(4, BLK, BLK)] * 2, [PANEL], (table, *panel, *quarters), after)


def to_in_tiles(table, panel, quarters, after):
    n = len(panel)

    def body(table_ref, *refs):
        chunks, panel_ref = refs[n + 4 : -1], refs[-1]
        fill_panel(panel_ref, table_ref, refs[n : n + 4])
        for k, ref in enumerate(chunks):
            for j in range(2):
                put = functools.partial(ref.__setitem__, j)
                tile(table_ref, (table_ref[CAP] + k) % 4 * 2 + j, windows(refs[:n]), panel_ref, True, put)

    return call(body, [(2, BLK, BLK)] * 4, [PANEL], (table, *panel, *quarters), after)


def in_order(table, parts):
    def body(table_ref, own, before, after, across_out, across_in, out_grad, in_grad):
        def at(k):
            return pl.ds((table_ref[CAP] + k) % 4 * 2, 2)

        for k, ref in ((0, own), (3, before), (1, after)):
            out_grad[at(k)] = ref[:2]
            in_grad[at(k)] = ref[2:]
        out_grad[at(2)] = across_out[...]
        in_grad[at(2)] = across_in[...]

    return call(body, [(CAP, BLK, BLK)] * 2, [], (table, *parts))


A = (2.0 / np.pi) ** 0.5
B = 0.044715


def gated(pair, other, after=()):
    def body(pair_ref, other_ref, *out_refs):
        v = add(pair_ref[...], other_ref[...])
        gate = (0.5 * v * (1.0 + jnp.tanh(A * (v + B * v * v * v)))).astype(BF16)
        for i, ref in enumerate(out_refs):
            ref[...] = gate[i * GROUP : (i + 1) * GROUP]

    return call(body, [(GROUP, HIDDEN)] * 2, [], (pair, other), after, False)


def ungated(pair, other, back_pair, back_other, after):
    def body(pair_ref, other_ref, back_ref, back_other_ref, *out_refs):
        v, g = add(pair_ref[...], other_ref[...]), add(back_ref[...], back_other_ref[...])
        t = jnp.tanh(A * (v + B * v * v * v))
        slope = 0.5 * (1.0 + t) + 0.5 * v * (1.0 - t * t) * (A * (1.0 + 3.0 * B * v * v))
        grad = (g * slope).astype(BF16)
        for i, ref in enumerate(out_refs):
            ref[...] = grad[i * GROUP : (i + 1) * GROUP]

    return call(body, [(GROUP, HIDDEN)] * 2, [], (pair, other, back_pair, back_other), after, False)


def chip_sum(quarters):
    arrived = swap_core(quarters[2:])
    kept = jnp.concatenate(quarters[:2], axis=0)
    return add(kept, jnp.concatenate(arrived, axis=0)).astype(BF16)


def after(value, *others):
    return lax.optimization_barrier((value, others))[0]


def per_device(activations, in_tiles, out_tiles, block_slots, out_cotangent):
    places = jnp.stack([lax.axis_index("dp"), lax.axis_index("row") % 2]).astype(jnp.int32)
    table = jnp.concatenate([block_slots[0, 0], places])
    in_tiles, out_tiles = in_tiles[0, 0], out_tiles[0, 0]

    near = gather_z(activations)
    near_cots = gather_z(after(out_cotangent, near))
    acts, cots = gather_x(near), gather_x(near_cots)

    pair = chip_sum(to_hidden(table, acts, in_tiles, True, one=False))
    other = swap_z(pair)
    gate = gated(pair, other)
    gate = *gate, *swap_core(gate)
    out_parts = to_features(table, gate, out_tiles, True)
    back_pair = chip_sum(to_hidden(table, cots, out_tiles, False, out_parts[:1], one=True))
    out_grad = to_out_tiles(table, cots, gate, (back_pair,))
    grad = ungated(pair, other, back_pair, swap_z(back_pair), out_grad[:1])
    grad = *grad, *swap_core(grad)
    out_total = add(*scatter_x(*out_parts)[0]).astype(BF16)
    act_parts = to_features(table, grad, in_tiles, False)
    chunks = to_in_tiles(table, acts, grad, act_parts[:1])
    act_terms, sent = scatter_x(*act_parts, chunks[:1])
    out_sum = halve_dp(*out_grad, act_parts[0])
    in_sum = sum_dp(after(chunks, sent, out_total))
    grads = jnp.concatenate([out_sum, in_sum], axis=0)
    outs = scatter_z(*pack(out_total, *act_terms))
    out_grad, in_grad = spread_dp(table, grads)
    outs = add(*after(outs, out_grad)).astype(BF16)
    return outs[0], outs[1], in_grad[None, None], out_grad[None, None]


def solution(mesh):
    in_specs = (
        P(("col", "dp"), "row"),
        P("row", "col", None, None, None),
        P("row", "col", None, None, None),
        P("row", "col", None),
        P(("col", "dp"), "row"),
    )
    out_specs = (
        P(("col", "dp"), "row"),
        P(("col", "dp"), "row"),
        P("row", "col", None, None, None),
        P("row", "col", None, None, None),
    )
    return jax.shard_map(
        per_device, mesh=mesh, in_specs=in_specs, out_specs=out_specs, check_vma=False
    )
```
